32 devices in a mesh: mode: 4 (over z), gx: 4 (over x, core), gy: 2 (over y).
Axes of the slice: x: 2, y: 2, z: 4, core: 2. Of those that a mesh axis runs over, the one named last changes fastest.
Arguments:
- values: float32 [8, 40, 160, 8, 128], P('mode', 'gx', 'gy'), may hold values from -6 to 6
- coef_table: float32 [3, 4], replicated, may hold values from -1 to 1
- mode_coef: int32 [8], P('mode'), may hold values from 0 to 3
- switch_mask: int32 [8, 8], replicated, may hold values 0 or 1
- switch_cost: float32 [8, 8], replicated, may hold values from 0 to 1
Outputs:
- sectioned: float32 [8, 40, 160, 2, 128], P('mode', 'gx', 'gy')
The draws below stay inside these ranges and needn't reach their ends.
All inputs are finite; a program needn't handle non-finite values.
Results may differ from the reference program's by a relative error of at most 0.0003.
Values sent between devices are 32-bit elements; how exact they have to be, the bound alone decides.
A program may use at most 128 MiB of HBM per device.

```python
import jax
import jax.numpy as jnp
from jax import lax

N3 = 128
KINDS = 4
MODES = 8
NX1 = 40
NX2 = 160
DEPTH = 8


def place_ends(values, own_key, low, high):
    dims = values.shape
    index_at = [jax.random.randint(jax.random.fold_in(own_key, axis), (), 0, dims[axis]) for axis in range(len(dims))]
    values = values.at[tuple(index_at)].set(low)
    longest = dims.index(max(dims))
    index_at[longest] = (index_at[longest] + 1) % dims[longest]
    return values.at[tuple(index_at)].set(high)


def shard_levels(stream_key, dims, split, smallest, high):
    gain = 1.0
    for axis_at, parts in split:
        heights = jax.random.uniform(jax.random.fold_in(jax.random.fold_in(stream_key, 6), axis_at), (parts,), jnp.float32, smallest / len(split), high / len(split))
        gain = gain * jnp.repeat(jnp.exp(heights), dims[axis_at] // parts).reshape((-1,) + (1,) * (len(dims) - 1 - axis_at))
    return gain


def centred(rng, extent, width, reach, pieces=(), held_as=jnp.bfloat16):
    values = width * jax.random.normal(rng, extent, jnp.float32)
    if pieces:
        values = values * shard_levels(rng, extent, pieces, -0.22, 0.18)
    return jnp.clip(values, -reach, reach).astype(held_as)


def setup_inputs(seed: int = 0) -> dict:
    splits = jax.random.split(jax.random.key(seed), 6)
    return {
        "values": centred(splits[0], (MODES, NX1, NX2, DEPTH, N3), 1.0, 6.0, ((0, 4), (1, 4), (2, 2)), jnp.float32),
        "coef_table": jnp.clip(jax.random.uniform(splits[1], (3, KINDS), jnp.float32, -1.0, 1.0), -1.0, 1.0),
        "mode_coef": place_ends(jax.random.randint(splits[2], (MODES,), 0, KINDS), jax.random.fold_in(splits[2], 1), 0, KINDS - 1).astype(jnp.int32),
        "switch_mask": place_ends((jax.random.randint(splits[3], (MODES, MODES), 0, 4) < 1).astype(jnp.int32), jax.random.fold_in(splits[3], 1), 0, 1),
        "switch_cost": jnp.clip(jax.random.uniform(splits[4], (MODES, MODES), jnp.float32, 0.0, 1.0), 0.0, 1.0),
    }


epsilon = 1e-6
time_step = 0.1


def weno_mix(d_one, d_two, d_three, d_four, d_five):
    smooth_one = 13.0 / 12.0 * (d_one - 2.0 * d_two + d_three) ** 2 + 0.25 * (d_one - 4.0 * d_two + 3.0 * d_three) ** 2
    smooth_two = 13.0 / 12.0 * (d_two - 2.0 * d_three + d_four) ** 2 + 0.25 * (d_two - d_four) ** 2
    smooth_three = 13.0 / 12.0 * (d_three - 2.0 * d_four + d_five) ** 2 + 0.25 * (3.0 * d_three - 4.0 * d_four + d_five) ** 2
    weight_one = 0.1 / (epsilon + smooth_one) ** 2
    weight_two = 0.6 / (epsilon + smooth_two) ** 2
    weight_three = 0.3 / (epsilon + smooth_three) ** 2
    weight_sum = weight_one + weight_two + weight_three
    mixed = weight_one * (d_one / 3.0 - 7.0 * d_two / 6.0 + 11.0 * d_three / 6.0)
    mixed = mixed + weight_two * (-d_two / 6.0 + 5.0 * d_three / 6.0 + d_four / 3.0)
    mixed = mixed + weight_three * (d_three / 3.0 + 5.0 * d_four / 6.0 - d_five / 6.0)
    return mixed / weight_sum


def weno_pair(extended, axis_no, length):
    spread = lax.slice_in_dim(extended, 1, length + 6, axis=axis_no) - lax.slice_in_dim(extended, 0, length + 5, axis=axis_no)
    shifted = [lax.slice_in_dim(spread, k, k + length, axis=axis_no) for k in range(6)]
    minus_side = weno_mix(shifted[0], shifted[1], shifted[2], shifted[3], shifted[4])
    plus_side = weno_mix(shifted[5], shifted[4], shifted[3], shifted[2], shifted[1])
    return minus_side, plus_side


def section_update(centre, slopes, shift_c, turn_raw, accel_c):
    heading = 2.0 * jnp.pi * lax.broadcasted_iota(jnp.float32, centre.shape, centre.ndim - 1) / centre.shape[-1]
    speed_value = 1.0 + 0.5 * lax.broadcasted_iota(jnp.float32, centre.shape, centre.ndim - 2)
    top_speed = 1.0 + 0.5 * (centre.shape[-2] - 1)
    turn_c = 0.5 + jnp.abs(turn_raw)
    means = [0.5 * (slopes[k][0] + slopes[k][1]) for k in range(4)]
    jumps = [slopes[k][1] - slopes[k][0] for k in range(4)]
    hamiltonian = means[0] * (speed_value * jnp.cos(heading) - shift_c) + means[1] * speed_value * jnp.sin(heading)
    hamiltonian = hamiltonian + turn_c * jnp.abs(means[2]) + accel_c * means[3]
    dissipation = (top_speed + jnp.abs(shift_c)) * jumps[0] + top_speed * jumps[1] + turn_c * jumps[2] + jnp.abs(accel_c) * jumps[3]
    return centre - time_step * (hamiltonian - 0.5 * dissipation)


def mode_section(mode_item):
    mode_block, coefficients = mode_item
    planes = mode_block.shape[2] - 6
    centre = mode_block[:, :, 3:3 + planes]
    wide_one = jnp.pad(centre, ((3, 3), (0, 0), (0, 0), (0, 0)))
    wide_two = jnp.pad(centre, ((0, 0), (3, 3), (0, 0), (0, 0)))
    wide_three = jnp.concatenate([centre[..., -3:], centre, centre[..., :3]], axis=3)
    slopes = [weno_pair(wide_one, 0, centre.shape[0]), weno_pair(wide_two, 1, centre.shape[1]),
              weno_pair(wide_three, 3, centre.shape[3]), weno_pair(mode_block, 2, planes)]
    return section_update(centre, slopes, coefficients[0], coefficients[1], coefficients[2])


def reference(values, coef_table, mode_coef, switch_mask, switch_cost):
    picked = jnp.take(coef_table, mode_coef, axis=1).T
    updated = lax.map(mode_section, (values, picked))

    def switch_one(target):
        def absorb(source, running):
            allowed = (switch_mask[target, source] == 1) & (source != target)
            candidate = updated[source] + switch_cost[target, source]
            return jnp.where(allowed, jnp.minimum(running, candidate), running)
        return lax.fori_loop(0, MODES, absorb, updated[target])

    return lax.map(switch_one, jnp.arange(MODES, dtype=jnp.int32))
```

```python
import functools

import jax
import jax.numpy as jnp
from jax import lax
from jax.experimental import pallas as pl
from jax.experimental.pallas import tpu as pltpu
from jax.sharding import PartitionSpec as P

epsilon = 1e-06
time_step = 0.1
MESH = pl.DeviceIdType.MESH
REACH = 3
PAD = 8
TILE = 8
BLOCK = 16
OUT_LAG = 4


def line_place(n):
    z = lax.axis_index("mode")
    half = n // 2
    left = z < half
    h = jnp.where(left, z, n - 1 - z)
    return z, left, h


def plan_kernel(n, per, reduce, mask, cost, table, kinds, coef, send, take, rank):
    z, left, h = line_place(n)
    half = n // 2
    side = per * half
    big = jnp.float32(jnp.inf)

    def mode_of(on_left, i):
        dev = i // per
        return per * jnp.where(on_left, dev, n - 1 - dev) + i % per

    def edge(target, source):
        ok = (mask[target, source] == 1) & (target != source)
        return jnp.where(ok, cost[target, source], big)

    for m in range(per):
        kind = kinds[m]
        for j in range(3):
            coef[m, j] = table[j, kind]

    def cover(from_left):
        rows = []
        for t in range(side):
            bits = jnp.int32(0)
            for i in range(side):
                hit = mask[mode_of(~from_left, t), mode_of(from_left, i)] == 1
                bits = bits + jnp.where(hit, jnp.int32(1 << i), jnp.int32(0))
            rows.append(bits)

        def size_of(chosen):
            total = jnp.int32(0)
            for i in range(side):
                total = total + ((chosen >> i) & 1)
            for t in range(side):
                total = total + jnp.where((rows[t] & ~chosen) != 0, 1, 0)
            return total

        everything = jnp.int32((1 << side) - 1)
        if not reduce:
            return rows, everything, jnp.int32(side)

        def better(s, best):
            size = size_of(s)
            win = size < best[1]
            return jnp.where(win, s, best[0]), jnp.where(win, size, best[1])

        chosen, size = lax.fori_loop(
            0, (1 << side) - 1, better, (everything, jnp.int32(side))
        )
        return rows, chosen, size

    for j in range(side):
        for i in range(side):
            send[j, i] = big
    for row in range(per + side):
        for col in range(per + 2 * side):
            take[row, col] = big

    own = [mode_of(left, per * h + m) for m in range(per)]
    for m in range(per):
        for o in range(per):
            take[m, o] = edge(own[m], own[o])
        for i in range(side - per):
            take[m, per + i] = edge(own[m], mode_of(left, i))
    for j in range(side - per):
        for o in range(per):
            take[per + j, o] = edge(mode_of(left, j), own[o])

    rows_out, set_out, size_out = cover(left)
    rows_in, set_in, size_in = cover(~left)
    rank[0] = jnp.maximum(size_out, size_in)

    @pl.when(h < half - 1)
    def _():
        for j in range(side):
            for m in range(per):
                take[m, per + side + j] = jnp.where(j == per * h + m, 0.0, big)
            if j < side - per:
                take[per + j, per + side + j] = 0.0

    @pl.when(h == half - 1)
    def _():
        place = jnp.int32(0)
        for i in range(side):
            inside = ((set_out >> i) & 1) == 1
            at = place

            @pl.when(inside)
            def _():
                send[at, i] = 0.0

            place = place + jnp.where(inside, 1, 0)
        for t in range(side):
            inside = (rows_out[t] & ~set_out) != 0
            at = place

            @pl.when(inside)
            def _():
                for i in range(side):
                    send[at, i] = edge(mode_of(~left, t), mode_of(left, i))

            place = place + jnp.where(inside, 1, 0)
        row_of = [per + t if t < side - per else t - (side - per) for t in range(side)]
        place = jnp.int32(0)
        for i in range(side):
            inside = ((set_in >> i) & 1) == 1
            at = place

            @pl.when(inside)
            def _():
                for t in range(side):
                    take[row_of[t], per + side + at] = edge(mode_of(left, t), mode_of(~left, i))

            place = place + jnp.where(inside, 1, 0)
        for t in range(side):
            inside = (rows_in[t] & ~set_in) != 0
            at = place

            @pl.when(inside)
            def _():
                take[row_of[t], per + side + at] = 0.0

            place = place + jnp.where(inside, 1, 0)


def weno_cells(u, count):
    d = [u[k + 1] - u[k] for k in range(count + 5)]
    e = [d[k + 1] - d[k] for k in range(count + 4)]
    e3 = [3.0 * e[k] for k in range(count + 4)]
    fs = [e[k + 1] - e[k] for k in range(count + 3)]
    g = [(13.0 / 3.0) * (f * f) + 4.0 * epsilon for f in fs]

    def squared(x, k):
        s = g[k] + x * x
        return s * s

    first = {k: squared(e[k] - e3[k + 1], k) for k in range(0, count + 1)}
    second = {k: squared(e[k] + e[k + 1], k) for k in range(1, count + 2)}
    third = {k: squared(e3[k] - e[k + 1], k) for k in range(2, count + 3)}

    def mix(a, b, c, x, y, w):
        wa = b * c
        wb = 6.0 * (a * c)
        wc = 3.0 * (a * b)
        return (wa * x + wb * y + wc * w) * pl.reciprocal(6.0 * (wa + wb + wc), approx=True)

    out = []
    for i in range(count):
        minus = d[i + 2] + mix(
            first[i],
            second[i + 1],
            third[i + 2],
            5.0 * e[i + 1] - 2.0 * e[i],
            e[i + 1] + 2.0 * e[i + 2],
            4.0 * e[i + 2] - e[i + 3],
        )
        plus = d[i + 3] - mix(
            third[i + 3],
            second[i + 2],
            first[i + 1],
            5.0 * e[i + 3] - 2.0 * e[i + 4],
            e[i + 3] + 2.0 * e[i + 2],
            4.0 * e[i + 2] - e[i + 1],
        )
        out.append((minus, plus))
    return out


def section_kernel(
    n, gx_count, gy_count, slots,
    coef, send_tab, take_tab, vals_hbm, out,
    vals, cells, fresh, outer_rx, inner_rx, in_slot, out_slot,
    load_sem, halo_send, halo_recv, in_send, in_recv, out_send, out_recv,
):
    per, rows, deep, lanes = vals.shape
    planes = cells.shape[0]
    cols = fresh.shape[3]
    depth = deep // cols
    tiles = cols // TILE
    half = n // 2
    side = per * half
    z, left, h = line_place(n)
    gx, gy = lax.axis_index("gx"), lax.axis_index("gy")
    inner_z = jnp.where(left, z + 1, z - 1)
    outer_z = jnp.where(left, z - 1, z + 1)

    loads = [
        pltpu.make_async_copy(vals_hbm.at[m], vals.at[m], load_sem.at[m]) for m in range(per)
    ]
    for copy in loads:
        copy.start()

    has = [gx > 0, gx < gx_count - 1, gy > 0, gy < gy_count - 1]
    barrier = pltpu.get_barrier_semaphore()
    peers = [
        (has[0], {"gx": gx - 1}),
        (has[1], {"gx": gx + 1}),
        (has[2], {"gy": gy - 1}),
        (has[3], {"gy": gy + 1}),
        (h > 0, {"mode": outer_z}),
        (h >= 0, {"mode": inner_z}),
    ]
    for there, who in peers:
        @pl.when(there)
        def _():
            pl.semaphore_signal(barrier, inc=1, device_id=who, device_id_type=MESH)

    for k, (there, lo) in enumerate([(has[0], 0), (has[1], REACH + rows)]):
        @pl.when(~there)
        def _():
            cells[:, :, lo : lo + REACH] = jnp.zeros(
                (planes, per, REACH) + cells.shape[3:], jnp.float32
            )
    for k, (there, lo) in enumerate([(has[2], 0), (has[3], PAD + cols)]):
        @pl.when(~there)
        def _():
            cells[:, :, REACH : REACH + rows, lo : lo + PAD] = jnp.zeros(
                (planes, per, rows, PAD, lanes), jnp.float32
            )

    for m in range(per):
        loads[m].wait()

        def pack(i, carry, m=m):
            for p in range(planes):
                cells[p, m, REACH + i, PAD : PAD + cols] = vals[
                    m, i, pl.ds(REACH + p, cols, stride=depth)
                ]
            return carry

        lax.fori_loop(0, rows, pack, 0)

    met = sum(there.astype(jnp.int32) for there, _ in peers)
    pl.semaphore_wait(barrier, met)

    inside = slice(PAD, PAD + cols)
    body_rows = slice(REACH, REACH + rows)

    def cut(r, c):
        return cells.at[:, :, r.start : r.stop, c.start : c.stop]

    spans = [
        (cut(slice(REACH, 2 * REACH), inside), cut(slice(REACH + rows, 2 * REACH + rows), inside)),
        (cut(slice(rows, REACH + rows), inside), cut(slice(0, REACH), inside)),
        (cut(body_rows, slice(PAD, 2 * PAD)), cut(body_rows, slice(PAD + cols, 2 * PAD + cols))),
        (cut(body_rows, slice(cols, PAD + cols)), cut(body_rows, slice(0, PAD))),
    ]
    halos = [
        pltpu.make_async_remote_copy(
            src_ref=src,
            dst_ref=dst,
            send_sem=halo_send.at[k],
            recv_sem=halo_recv.at[k],
            device_id=peers[k][1],
            device_id_type=MESH,
        )
        for k, (src, dst) in enumerate(spans)
    ]
    for k in (2, 3, 1, 0):
        @pl.when(has[k])
        def _():
            halos[k].start()

    for k, there in ((3, has[2]), (2, has[3])):
        @pl.when(there)
        def _():
            halos[k].wait_recv()

    lane = lax.broadcasted_iota(jnp.int32, (TILE, lanes), 1).astype(jnp.float32)
    heading = 2.0 * jnp.pi * lane / lanes
    cosine, sine = jnp.cos(heading), jnp.sin(heading)
    top = 1.0 + 0.5 * (planes - 1)

    def row_at(s):
        return lax.rem(s + REACH, rows)

    def update_row(row):
        for m in range(per):
            shift, raw, accel = coef[m, 0], coef[m, 1], coef[m, 2]
            turn = 0.5 + jnp.abs(raw)
            side_one = 0.5 * (top + jnp.abs(shift))
            side_four = 0.5 * jnp.abs(accel)

            def tile(t, carry):
                base = pl.multiple_of(t * TILE, TILE)
                stack = [
                    vals[m, row, pl.ds(base * depth + j, TILE, stride=depth)]
                    for j in range(planes + 2 * REACH)
                ]
                four = weno_cells(stack, planes)
                for p in range(planes):
                    speed = 1.0 + 0.5 * p
                    centre = stack[REACH + p]
                    lane_shift = [
                        centre if k == REACH else pltpu.roll(centre, (REACH - k) % lanes, 1)
                        for k in range(2 * REACH + 1)
                    ]
                    one = weno_cells(
                        [
                            cells[p, m, row + k, pl.ds(base + PAD, TILE)]
                            for k in range(2 * REACH + 1)
                        ],
                        1,
                    )[0]
                    two = weno_cells(
                        [
                            cells[p, m, row + REACH, pl.ds(base + (PAD - REACH + k), TILE)]
                            for k in range(2 * REACH + 1)
                        ],
                        1,
                    )[0]
                    three = weno_cells(lane_shift, 1)[0]
                    total = (0.5 * (speed * cosine - shift)) * (one[0] + one[1])
                    total = total - side_one * (one[1] - one[0])
                    total = total + (0.5 * speed * sine) * (two[0] + two[1])
                    total = total - (0.5 * top) * (two[1] - two[0])
                    total = total + (0.5 * turn) * (
                        jnp.abs(three[0] + three[1]) - (three[1] - three[0])
                    )
                    total = total + (0.5 * accel) * (four[p][0] + four[p][1])
                    total = total - side_four * (four[p][1] - four[p][0])
                    fresh[row, m, p, pl.ds(base, TILE)] = centre - time_step * total
                return carry

            lax.fori_loop(0, tiles, tile, 0)

    def inward_copies(hh, row):
        if hh == half - 1:
            return [
                pltpu.make_async_remote_copy(
                    src_ref=in_slot.at[row],
                    dst_ref=inner_rx.at[row, pl.ds(0, slots)],
                    send_sem=in_send.at[row, 0],
                    recv_sem=out_recv.at[row],
                    device_id={"mode": inner_z},
                    device_id_type=MESH,
                )
            ]
        copies = [
            pltpu.make_async_remote_copy(
                src_ref=fresh.at[row],
                dst_ref=outer_rx.at[row, pl.ds(per * hh, per)],
                send_sem=in_send.at[row, 0],
                recv_sem=in_recv.at[row, 0],
                device_id={"mode": inner_z},
                device_id_type=MESH,
            )
        ]
        if hh > 0:
            copies.append(
                pltpu.make_async_remote_copy(
                    src_ref=outer_rx.at[row, pl.ds(0, per * hh)],
                    dst_ref=outer_rx.at[row, pl.ds(0, per * hh)],
                    send_sem=in_send.at[row, 1],
                    recv_sem=in_recv.at[row, 1],
                    device_id={"mode": inner_z},
                    device_id_type=MESH,
                )
            )
        return copies

    def outward_copy(hh, row):
        return pltpu.make_async_remote_copy(
            src_ref=out_slot.at[row, pl.ds(0, per * hh)],
            dst_ref=inner_rx.at[row, pl.ds(0, per * hh)],
            send_sem=out_send.at[row],
            recv_sem=out_recv.at[row],
            device_id={"mode": outer_z},
            device_id_type=MESH,
        )

    def least(start, pairs):
        best = start
        for value, weight in pairs:
            best = value + weight if best is None else jnp.minimum(best, value + weight)
        return best

    def each_stage(body):
        for hh in range(half):
            @pl.when(h == hh)
            def _():
                body(hh)

    blocks = cols // BLOCK

    def inward(row):
        def stage(hh):
            if hh > 0:
                for copy in inward_copies(hh - 1, row):
                    copy.wait_recv()
            if hh == half - 1:
                def block(b, carry):
                    span = pl.ds(pl.multiple_of(b * BLOCK, BLOCK), BLOCK)
                    for p in range(planes):
                        given = [outer_rx[row, i, p, span] for i in range(per * hh)]
                        given += [fresh[row, m, p, span] for m in range(per)]
                        for j in range(slots):
                            in_slot[row, j, p, span] = least(
                                None, [(given[i], send_tab[j, i]) for i in range(side)]
                            )
                    return carry

                lax.fori_loop(0, blocks, block, 0)
            for copy in inward_copies(hh, row):
                copy.start()

        each_stage(stage)

    def outward(row):
        def stage(hh):
            mid = hh == half - 1
            arrived = slots if mid else per * (hh + 1)
            if mid:
                inward_copies(hh, row)[0].wait_recv()
            else:
                outward_copy(hh + 1, row).wait_recv()

            def block(b, carry):
                start = pl.multiple_of(b * BLOCK, BLOCK)
                span = pl.ds(start, BLOCK)
                for p in range(planes):
                    own = [fresh[row, m, p, span] for m in range(per)]
                    outer = [outer_rx[row, i, p, span] for i in range(per * hh)]
                    inner = [inner_rx[row, j, p, span] for j in range(arrived)]
                    base = per + side
                    for j in range(per * hh):
                        pairs = [(own[m], take_tab[per + j, m]) for m in range(per)]
                        if mid:
                            pairs += [
                                (inner[k], take_tab[per + j, base + k]) for k in range(arrived)
                            ]
                            out_slot[row, j, p, span] = least(None, pairs)
                        else:
                            out_slot[row, j, p, span] = least(inner[j], pairs)
                    for m in range(per):
                        pairs = [(own[o], take_tab[m, o]) for o in range(per) if o != m]
                        pairs += [(outer[i], take_tab[m, per + i]) for i in range(per * hh)]
                        if mid:
                            pairs += [(inner[k], take_tab[m, base + k]) for k in range(arrived)]
                            best = least(own[m], pairs)
                        else:
                            best = least(jnp.minimum(own[m], inner[per * hh + m]), pairs)
                        out[m, row, pl.ds(start * planes + p, BLOCK, stride=planes)] = best
                return carry

            lax.fori_loop(0, blocks, block, 0)
            if hh > 0:
                outward_copy(hh, row).start()

        each_stage(stage)

    def step(s, carry):
        @pl.when((s == rows - 2 * REACH) & has[1])
        def _():
            halos[0].wait_recv()

        @pl.when((s == rows - REACH) & has[0])
        def _():
            halos[1].wait_recv()

        update_row(row_at(s))
        inward(row_at(s))

        @pl.when(s >= OUT_LAG)
        def _():
            outward(row_at(s - OUT_LAG))

        return carry

    lax.fori_loop(0, rows, step, 0)

    def rest(s, carry):
        outward(row_at(s))
        return carry

    lax.fori_loop(rows - OUT_LAG, rows, rest, 0)

    for k in range(4):
        @pl.when(has[k])
        def _():
            halos[k].wait_send()

    def finish(row, carry):
        def stage(hh):
            for copy in inward_copies(hh, row):
                copy.wait_send()
            if hh > 0:
                outward_copy(hh, row).wait_send()

        each_stage(stage)
        return carry

    lax.fori_loop(0, rows, finish, 0)


def smem():
    return pl.BlockSpec(memory_space=pltpu.SMEM)


def shards(n, gx_count, gy_count, values, coef_table, mode_coef, switch_mask, switch_cost):
    per, rows, cols, depth, lanes = values.shape
    planes = depth - 2 * REACH
    side = per * (n // 2)
    f32 = jnp.float32
    coef, send_tab, take_tab, rank = pl.pallas_call(
        functools.partial(plan_kernel, n, per, False),
        out_shape=(
            jax.ShapeDtypeStruct((per, 3), f32),
            jax.ShapeDtypeStruct((side, side), f32),
            jax.ShapeDtypeStruct((per + side, per + 2 * side), f32),
            jax.ShapeDtypeStruct((1,), jnp.int32),
        ),
        in_specs=[smem()] * 4,
        out_specs=(smem(),) * 4,
        name="plan",
    )(switch_mask, switch_cost, coef_table, mode_coef)
    slots = side
    piece = (planes, cols, lanes)
    dma = pltpu.SemaphoreType.DMA
    out = pl.pallas_call(
        functools.partial(section_kernel, n, gx_count, gy_count, slots),
        out_shape=jax.ShapeDtypeStruct((per, rows, cols * planes, lanes), f32),
        in_specs=[smem()] * 3 + [pl.BlockSpec(memory_space=pl.ANY)],
        out_specs=pl.BlockSpec(memory_space=pltpu.VMEM),
        scratch_shapes=[
            pltpu.VMEM((per, rows, cols * depth, lanes), f32),
            pltpu.VMEM((planes, per, rows + 2 * REACH, cols + 2 * PAD, lanes), f32),
            pltpu.VMEM((rows, per) + piece, f32),
            pltpu.VMEM((rows, max(side - per, 1)) + piece, f32),
            pltpu.VMEM((rows, side) + piece, f32),
            pltpu.VMEM((rows, slots) + piece, f32),
            pltpu.VMEM((rows, max(side - per, 1)) + piece, f32),
            dma((per,)),
            dma((4,)),
            dma((4,)),
            dma((rows, 2)),
            dma((rows, 2)),
            dma((rows,)),
            dma((rows,)),
        ],
        compiler_params=pltpu.CompilerParams(
            collective_id=0, has_side_effects=True, vmem_limit_bytes=58 * 1024 * 1024
        ),
        name="section",
    )(coef, send_tab, take_tab, values.reshape(per, rows, cols * depth, lanes))
    return out.reshape(per, rows, cols, planes, lanes)


def solution(mesh):
    in_specs = (P("mode", "gx", "gy", None, None), P(), P("mode"), P(), P())
    out_specs = P("mode", "gx", "gy", None, None)
    body = functools.partial(shards, mesh.shape["mode"], mesh.shape["gx"], mesh.shape["gy"])
    return jax.shard_map(body, mesh=mesh, in_specs=in_specs, out_specs=out_specs, check_vma=False)
```

```python
import functools

import jax
import jax.numpy as jnp
from jax import lax
from jax.experimental import pallas as pl
from jax.experimental.pallas import tpu as pltpu
from jax.sharding import PartitionSpec as P

epsilon = 1e-06
time_step = 0.1
MESH = pl.DeviceIdType.MESH
REACH = 3
PAD = 8
TILE = 8
BLOCK = 16
OUT_LAG = 3


def line_place(n):
    z = lax.axis_index("mode")
    half = n // 2
    left = z < half
    h = jnp.where(left, z, n - 1 - z)
    return z, left, h


def plan_kernel(n, per, mask, cost, table, kinds, coef, send, take, rank):
    z, left, h = line_place(n)
    half = n // 2
    side = per * half
    big = jnp.float32(jnp.inf)

    def mode_of(on_left, i):
        dev = i // per
        return per * jnp.where(on_left, dev, n - 1 - dev) + i % per

    def edge(target, source):
        ok = (mask[target, source] == 1) & (target != source)
        return jnp.where(ok, cost[target, source], big)

    for m in range(per):
        kind = kinds[m]
        for j in range(3):
            coef[m, j] = table[j, kind]

    def cover(from_left):
        rows = []
        for t in range(side):
            bits = jnp.int32(0)
            for i in range(side):
                hit = mask[mode_of(~from_left, t), mode_of(from_left, i)] == 1
                bits = bits + jnp.where(hit, jnp.int32(1 << i), jnp.int32(0))
            rows.append(bits)

        def size_of(chosen):
            total = jnp.int32(0)
            for i in range(side):
                total = total + ((chosen >> i) & 1)
            for t in range(side):
                total = total + jnp.where((rows[t] & ~chosen) != 0, 1, 0)
            return total

        everything = jnp.int32((1 << side) - 1)

        def better(s, best):
            size = size_of(s)
            win = size < best[1]
            return jnp.where(win, s, best[0]), jnp.where(win, size, best[1])

        chosen, size = lax.fori_loop(
            0, (1 << side) - 1, better, (everything, jnp.int32(side))
        )
        return rows, chosen, size

    for j in range(side):
        for i in range(side):
            send[j, i] = big
    for row in range(per + side):
        for col in range(per + 2 * side):
            take[row, col] = big

    own = [mode_of(left, per * h + m) for m in range(per)]
    for m in range(per):
        for o in range(per):
            take[m, o] = edge(own[m], own[o])
        for i in range(side - per):
            take[m, per + i] = edge(own[m], mode_of(left, i))
    for j in range(side - per):
        for o in range(per):
            take[per + j, o] = edge(mode_of(left, j), own[o])

    rows_out, set_out, size_out = cover(left)
    rows_in, set_in, size_in = cover(~left)
    rank[0] = jnp.maximum(size_out, size_in)

    @pl.when(h < half - 1)
    def _():
        for j in range(side):
            for m in range(per):
                take[m, per + side + j] = jnp.where(j == per * h + m, 0.0, big)
            if j < side - per:
                take[per + j, per + side + j] = 0.0

    @pl.when(h == half - 1)
    def _():
        place = jnp.int32(0)
        for i in range(side):
            inside = ((set_out >> i) & 1) == 1
            at = place

            @pl.when(inside)
            def _():
                send[at, i] = 0.0

            place = place + jnp.where(inside, 1, 0)
        for t in range(side):
            inside = (rows_out[t] & ~set_out) != 0
            at = place

            @pl.when(inside)
            def _():
                for i in range(side):
                    send[at, i] = edge(mode_of(~left, t), mode_of(left, i))

            place = place + jnp.where(inside, 1, 0)
        row_of = [per + t if t < side - per else t - (side - per) for t in range(side)]
        place = jnp.int32(0)
        for i in range(side):
            inside = ((set_in >> i) & 1) == 1
            at = place

            @pl.when(inside)
            def _():
                for t in range(side):
                    take[row_of[t], per + side + at] = edge(mode_of(left, t), mode_of(~left, i))

            place = place + jnp.where(inside, 1, 0)
        for t in range(side):
            inside = (rows_in[t] & ~set_in) != 0
            at = place

            @pl.when(inside)
            def _():
                take[row_of[t], per + side + at] = 0.0

            place = place + jnp.where(inside, 1, 0)


def weno_cells(u, count):
    d = [u[k + 1] - u[k] for k in range(count + 5)]
    e = [d[k + 1] - d[k] for k in range(count + 4)]
    e3 = [3.0 * e[k] for k in range(count + 4)]
    fs = [e[k + 1] - e[k] for k in range(count + 3)]
    g = [(13.0 / 3.0) * (f * f) + 4.0 * epsilon for f in fs]

    def squared(x, k):
        s = g[k] + x * x
        return s * s

    first = {k: squared(e[k] - e3[k + 1], k) for k in range(0, count + 1)}
    second = {k: squared(e[k] + e[k + 1], k) for k in range(1, count + 2)}
    third = {k: squared(e3[k] - e[k + 1], k) for k in range(2, count + 3)}

    def mix(a, b, c, x, y, w):
        wa = b * c
        wb = 6.0 * (a * c)
        wc = 3.0 * (a * b)
        return (wa * x + wb * y + wc * w) * pl.reciprocal(6.0 * (wa + wb + wc), approx=True)

    out = []
    for i in range(count):
        minus = d[i + 2] + mix(
            first[i],
            second[i + 1],
            third[i + 2],
            5.0 * e[i + 1] - 2.0 * e[i],
            e[i + 1] + 2.0 * e[i + 2],
            4.0 * e[i + 2] - e[i + 3],
        )
        plus = d[i + 3] - mix(
            third[i + 3],
            second[i + 2],
            first[i + 1],
            5.0 * e[i + 3] - 2.0 * e[i + 4],
            e[i + 3] + 2.0 * e[i + 2],
            4.0 * e[i + 2] - e[i + 1],
        )
        out.append((minus, plus))
    return out


def section_kernel(
    n, gx_count, gy_count, slots,
    coef, send_tab, take_tab, vals_hbm, out,
    vals, cells, fresh, outer_rx, inner_rx, in_slot, out_slot,
    load_sem, halo_send, halo_recv, in_send, in_recv, out_send, out_recv,
):
    per, rows, deep, lanes = vals.shape
    planes = cells.shape[0]
    cols = fresh.shape[3]
    depth = deep // cols
    tiles = cols // TILE
    half = n // 2
    side = per * half
    z, left, h = line_place(n)
    gx, gy = lax.axis_index("gx"), lax.axis_index("gy")
    inner_z = jnp.where(left, z + 1, z - 1)
    outer_z = jnp.where(left, z - 1, z + 1)

    loads = [
        pltpu.make_async_copy(vals_hbm.at[m], vals.at[m], load_sem.at[m]) for m in range(per)
    ]
    for copy in loads:
        copy.start()

    has = [gx > 0, gx < gx_count - 1, gy > 0, gy < gy_count - 1]
    barrier = pltpu.get_barrier_semaphore()
    peers = [
        (has[0], {"gx": gx - 1}),
        (has[1], {"gx": gx + 1}),
        (has[2], {"gy": gy - 1}),
        (has[3], {"gy": gy + 1}),
        (h > 0, {"mode": outer_z}),
        (h >= 0, {"mode": inner_z}),
    ]
    for there, who in peers:
        @pl.when(there)
        def _():
            pl.semaphore_signal(barrier, inc=1, device_id=who, device_id_type=MESH)

    for k, (there, lo) in enumerate([(has[0], 0), (has[1], REACH + rows)]):
        @pl.when(~there)
        def _():
            cells[:, :, lo : lo + REACH] = jnp.zeros(
                (planes, per, REACH) + cells.shape[3:], jnp.float32
            )
    for k, (there, lo) in enumerate([(has[2], 0), (has[3], PAD + cols)]):
        @pl.when(~there)
        def _():
            cells[:, :, REACH : REACH + rows, lo : lo + PAD] = jnp.zeros(
                (planes, per, rows, PAD, lanes), jnp.float32
            )

    for m in range(per):
        loads[m].wait()

        def pack(i, carry, m=m):
            for p in range(planes):
                cells[p, m, REACH + i, PAD : PAD + cols] = vals[
                    m, i, pl.ds(REACH + p, cols, stride=depth)
                ]
            return carry

        lax.fori_loop(0, rows, pack, 0)

    met = sum(there.astype(jnp.int32) for there, _ in peers)
    pl.semaphore_wait(barrier, met)

    inside = slice(PAD, PAD + cols)
    body_rows = slice(REACH, REACH + rows)

    def cut(r, c):
        return cells.at[:, :, r.start : r.stop, c.start : c.stop]

    spans = [
        (cut(slice(REACH, 2 * REACH), inside), cut(slice(REACH + rows, 2 * REACH + rows), inside)),
        (cut(slice(rows, REACH + rows), inside), cut(slice(0, REACH), inside)),
        (cut(body_rows, slice(PAD, 2 * PAD)), cut(body_rows, slice(PAD + cols, 2 * PAD + cols))),
        (cut(body_rows, slice(cols, PAD + cols)), cut(body_rows, slice(0, PAD))),
    ]
    halos = [
        pltpu.make_async_remote_copy(
            src_ref=src,
            dst_ref=dst,
            send_sem=halo_send.at[k],
            recv_sem=halo_recv.at[k],
            device_id=peers[k][1],
            device_id_type=MESH,
        )
        for k, (src, dst) in enumerate(spans)
    ]
    for k in (2, 3, 1, 0):
        @pl.when(has[k])
        def _():
            halos[k].start()

    for k, there in ((3, has[2]), (2, has[3])):
        @pl.when(there)
        def _():
            halos[k].wait_recv()

    lane = lax.broadcasted_iota(jnp.int32, (TILE, lanes), 1).astype(jnp.float32)
    heading = 2.0 * jnp.pi * lane / lanes
    cosine, sine = jnp.cos(heading), jnp.sin(heading)
    top = 1.0 + 0.5 * (planes - 1)

    def row_at(s):
        return lax.rem(s + REACH, rows)

    def update_row(row):
        for m in range(per):
            shift, raw, accel = coef[m, 0], coef[m, 1], coef[m, 2]
            turn = 0.5 + jnp.abs(raw)
            side_one = 0.5 * (top + jnp.abs(shift))
            side_four = 0.5 * jnp.abs(accel)

            def tile(t, carry):
                base = pl.multiple_of(t * TILE, TILE)
                stack = [
                    vals[m, row, pl.ds(base * depth + j, TILE, stride=depth)]
                    for j in range(planes + 2 * REACH)
                ]
                four = weno_cells(stack, planes)
                for p in range(planes):
                    speed = 1.0 + 0.5 * p
                    centre = stack[REACH + p]
                    lane_shift = [
                        centre if k == REACH else pltpu.roll(centre, (REACH - k) % lanes, 1)
                        for k in range(2 * REACH + 1)
                    ]
                    one = weno_cells(
                        [
                            cells[p, m, row + k, pl.ds(base + PAD, TILE)]
                            for k in range(2 * REACH + 1)
                        ],
                        1,
                    )[0]
                    two = weno_cells(
                        [
                            cells[p, m, row + REACH, pl.ds(base + (PAD - REACH + k), TILE)]
                            for k in range(2 * REACH + 1)
                        ],
                        1,
                    )[0]
                    three = weno_cells(lane_shift, 1)[0]
                    total = (0.5 * (speed * cosine - shift)) * (one[0] + one[1])
                    total = total - side_one * (one[1] - one[0])
                    total = total + (0.5 * speed * sine) * (two[0] + two[1])
                    total = total - (0.5 * top) * (two[1] - two[0])
                    total = total + (0.5 * turn) * (
                        jnp.abs(three[0] + three[1]) - (three[1] - three[0])
                    )
                    total = total + (0.5 * accel) * (four[p][0] + four[p][1])
                    total = total - side_four * (four[p][1] - four[p][0])
                    fresh[row, m, p, pl.ds(base, TILE)] = centre - time_step * total
                return carry

            lax.fori_loop(0, tiles, tile, 0)

    def inward_copies(hh, row):
        if hh == half - 1:
            return [
                pltpu.make_async_remote_copy(
                    src_ref=in_slot.at[row],
                    dst_ref=inner_rx.at[row, pl.ds(0, slots)],
                    send_sem=in_send.at[row, 0],
                    recv_sem=out_recv.at[row],
                    device_id={"mode": inner_z},
                    device_id_type=MESH,
                )
            ]
        copies = [
            pltpu.make_async_remote_copy(
                src_ref=fresh.at[row],
                dst_ref=outer_rx.at[row, pl.ds(per * hh, per)],
                send_sem=in_send.at[row, 0],
                recv_sem=in_recv.at[row, 0],
                device_id={"mode": inner_z},
                device_id_type=MESH,
            )
        ]
        if hh > 0:
            copies.append(
                pltpu.make_async_remote_copy(
                    src_ref=outer_rx.at[row, pl.ds(0, per * hh)],
                    dst_ref=outer_rx.at[row, pl.ds(0, per * hh)],
                    send_sem=in_send.at[row, 1],
                    recv_sem=in_recv.at[row, 1],
                    device_id={"mode": inner_z},
                    device_id_type=MESH,
                )
            )
        return copies

    def outward_copy(hh, row):
        return pltpu.make_async_remote_copy(
            src_ref=out_slot.at[row, pl.ds(0, per * hh)],
            dst_ref=inner_rx.at[row, pl.ds(0, per * hh)],
            send_sem=out_send.at[row],
            recv_sem=out_recv.at[row],
            device_id={"mode": outer_z},
            device_id_type=MESH,
        )

    def least(start, pairs):
        best = start
        for value, weight in pairs:
            best = value + weight if best is None else jnp.minimum(best, value + weight)
        return best

    def each_stage(body):
        for hh in range(half):
            @pl.when(h == hh)
            def _():
                body(hh)

    blocks = cols // BLOCK

    def inward(hh, row):
        if hh > 0:
            for copy in inward_copies(hh - 1, row):
                copy.wait_recv()
        if hh == half - 1:
            def block(b, carry):
                span = pl.ds(pl.multiple_of(b * BLOCK, BLOCK), BLOCK)
                for p in range(planes):
                    given = [outer_rx[row, i, p, span] for i in range(per * hh)]
                    given += [fresh[row, m, p, span] for m in range(per)]
                    for j in range(slots):
                        in_slot[row, j, p, span] = least(
                            None, [(given[i], send_tab[j, i]) for i in range(side)]
                        )
                return carry

            lax.fori_loop(0, blocks, block, 0)
        for copy in inward_copies(hh, row):
            copy.start()

    def outward(hh, row):
        mid = hh == half - 1
        arrived = slots if mid else per * (hh + 1)
        if mid:
            inward_copies(hh, row)[0].wait_recv()
        else:
            outward_copy(hh + 1, row).wait_recv()

        def block(b, carry):
            start = pl.multiple_of(b * BLOCK, BLOCK)
            span = pl.ds(start, BLOCK)
            for p in range(planes):
                own = [fresh[row, m, p, span] for m in range(per)]
                outer = [outer_rx[row, i, p, span] for i in range(per * hh)]
                inner = [inner_rx[row, j, p, span] for j in range(arrived)]
                base = per + side
                for j in range(per * hh):
                    pairs = [(own[m], take_tab[per + j, m]) for m in range(per)]
                    if mid:
                        pairs += [
                            (inner[k], take_tab[per + j, base + k]) for k in range(arrived)
                        ]
                        out_slot[row, j, p, span] = least(None, pairs)
                    else:
                        out_slot[row, j, p, span] = least(inner[j], pairs)
                for m in range(per):
                    pairs = [(own[o], take_tab[m, o]) for o in range(per) if o != m]
                    pairs += [(outer[i], take_tab[m, per + i]) for i in range(per * hh)]
                    if mid:
                        pairs += [(inner[k], take_tab[m, base + k]) for k in range(arrived)]
                        best = least(own[m], pairs)
                    else:
                        best = least(jnp.minimum(own[m], inner[per * hh + m]), pairs)
                    out[m, row, pl.ds(start * planes + p, BLOCK, stride=planes)] = best
            return carry

        lax.fori_loop(0, blocks, block, 0)
        if hh > 0:
            outward_copy(hh, row).start()

    in_lag = [hh for hh in range(half)]
    out_lag = [
        rows if hh == 0 and half > 1 else hh + OUT_LAG + 2 * (half - 1 - hh)
        for hh in range(half)
    ]

    def step(s, carry):
        @pl.when((s == rows - 2 * REACH) & has[1])
        def _():
            halos[0].wait_recv()

        @pl.when((s == rows - REACH) & has[0])
        def _():
            halos[1].wait_recv()

        @pl.when(s < rows)
        def _():
            update_row(row_at(s))

        def stage(hh):
            @pl.when((s >= in_lag[hh]) & (s < rows + in_lag[hh]))
            def _():
                inward(hh, row_at(s - in_lag[hh]))

            @pl.when((s >= out_lag[hh]) & (s < rows + out_lag[hh]))
            def _():
                outward(hh, row_at(s - out_lag[hh]))

        each_stage(stage)
        return carry

    lax.fori_loop(0, rows + max(in_lag + out_lag), step, 0)

    for k in range(4):
        @pl.when(has[k])
        def _():
            halos[k].wait_send()

    def finish(row, carry):
        def stage(hh):
            for copy in inward_copies(hh, row):
                copy.wait_send()
            if hh > 0:
                outward_copy(hh, row).wait_send()

        each_stage(stage)
        return carry

    lax.fori_loop(0, rows, finish, 0)


def smem():
    return pl.BlockSpec(memory_space=pltpu.SMEM)


def shards(n, gx_count, gy_count, values, coef_table, mode_coef, switch_mask, switch_cost):
    per, rows, cols, depth, lanes = values.shape
    planes = depth - 2 * REACH
    side = per * (n // 2)
    f32 = jnp.float32
    coef, send_tab, take_tab, rank = pl.pallas_call(
        functools.partial(plan_kernel, n, per),
        out_shape=(
            jax.ShapeDtypeStruct((per, 3), f32),
            jax.ShapeDtypeStruct((side, side), f32),
            jax.ShapeDtypeStruct((per + side, per + 2 * side), f32),
            jax.ShapeDtypeStruct((1,), jnp.int32),
        ),
        in_specs=[smem()] * 4,
        out_specs=(smem(),) * 4,
        name="plan",
    )(switch_mask, switch_cost, coef_table, mode_coef)
    piece = (planes, cols, lanes)
    dma = pltpu.SemaphoreType.DMA
    def section_with(slots, number):
        return pl.pallas_call(
            functools.partial(section_kernel, n, gx_count, gy_count, slots),
            out_shape=jax.ShapeDtypeStruct((per, rows, cols * planes, lanes), f32),
            in_specs=[smem()] * 3 + [pl.BlockSpec(memory_space=pl.ANY)],
            out_specs=pl.BlockSpec(memory_space=pltpu.VMEM),
            scratch_shapes=[
                pltpu.VMEM((per, rows, cols * depth, lanes), f32),
                pltpu.VMEM((planes, per, rows + 2 * REACH, cols + 2 * PAD, lanes), f32),
                pltpu.VMEM((rows, per) + piece, f32),
                pltpu.VMEM((rows, max(side - per, 1)) + piece, f32),
                pltpu.VMEM((rows, side) + piece, f32),
                pltpu.VMEM((rows, slots) + piece, f32),
                pltpu.VMEM((rows, max(side - per, 1)) + piece, f32),
                dma((per,)),
                dma((4,)),
                dma((4,)),
                dma((rows, 2)),
                dma((rows, 2)),
                dma((rows,)),
                dma((rows,)),
            ],
            compiler_params=pltpu.CompilerParams(
                collective_id=number, has_side_effects=True, vmem_limit_bytes=58 * 1024 * 1024
            ),
            name="section",
        )

    sizes = sorted({max(side // 2, 1), max(3 * side // 4, 1), side})
    pick = sum((rank[0] > size).astype(jnp.int32) for size in sizes[:-1])
    out = lax.switch(
        pick,
        [section_with(size, number) for number, size in enumerate(sizes)],
        coef,
        send_tab,
        take_tab,
        values.reshape(per, rows, cols * depth, lanes),
    )
    return out.reshape(per, rows, cols, planes, lanes)


def solution(mesh):
    in_specs = (P("mode", "gx", "gy", None, None), P(), P("mode"), P(), P())
    out_specs = P("mode", "gx", "gy", None, None)
    body = functools.partial(shards, mesh.shape["mode"], mesh.shape["gx"], mesh.shape["gy"])
    return jax.shard_map(body, mesh=mesh, in_specs=in_specs, out_specs=out_specs, check_vma=False)
```

```python
import functools

import jax
import jax.numpy as jnp
from jax import lax
from jax.experimental import pallas as pl
from jax.experimental.pallas import tpu as pltpu
from jax.sharding import PartitionSpec as P

epsilon = 1e-06
time_step = 0.1
MESH = pl.DeviceIdType.MESH
REACH = 3
PAD = 8
TILE = 8
BLOCK = 8
IN_LAG = 2
OUT_LAG = 6


def line_place(n):
    z = lax.axis_index("mode")
    half = n // 2
    left = z < half
    h = jnp.where(left, z, n - 1 - z)
    return z, left, h


def plan_kernel(n, per, mask, cost, table, kinds, coef, send, take, rank):
    z, left, h = line_place(n)
    half = n // 2
    side = per * half
    big = jnp.float32(jnp.inf)

    def mode_of(on_left, i):
        dev = i // per
        return per * jnp.where(on_left, dev, n - 1 - dev) + i % per

    def edge(target, source):
        ok = (mask[target, source] == 1) & (target != source)
        return jnp.where(ok, cost[target, source], big)

    for m in range(per):
        kind = kinds[m]
        for j in range(3):
            coef[m, j] = table[j, kind]

    def cover(from_left):
        rows = []
        for t in range(side):
            bits = jnp.int32(0)
            for i in range(side):
                hit = mask[mode_of(~from_left, t), mode_of(from_left, i)] == 1
                bits = bits + jnp.where(hit, jnp.int32(1 << i), jnp.int32(0))
            rows.append(bits)

        def size_of(chosen):
            total = jnp.int32(0)
            for i in range(side):
                total = total + ((chosen >> i) & 1)
            for t in range(side):
                total = total + jnp.where((rows[t] & ~chosen) != 0, 1, 0)
            return total

        everything = jnp.int32((1 << side) - 1)

        def better(s, best):
            size = size_of(s)
            win = size < best[1]
            return jnp.where(win, s, best[0]), jnp.where(win, size, best[1])

        chosen, size = lax.fori_loop(
            0, (1 << side) - 1, better, (everything, jnp.int32(side))
        )
        return rows, chosen, size

    for j in range(side):
        for i in range(side):
            send[j, i] = big
    for row in range(per + side):
        for col in range(per + 2 * side):
            take[row, col] = big

    own = [mode_of(left, per * h + m) for m in range(per)]
    for m in range(per):
        for o in range(per):
            take[m, o] = edge(own[m], own[o])
        for i in range(side - per):
            take[m, per + i] = edge(own[m], mode_of(left, i))
    for j in range(side - per):
        for o in range(per):
            take[per + j, o] = edge(mode_of(left, j), own[o])

    rows_out, set_out, size_out = cover(left)
    rows_in, set_in, size_in = cover(~left)
    rank[0] = jnp.maximum(size_out, size_in)

    @pl.when(h < half - 1)
    def _():
        for j in range(side):
            for m in range(per):
                take[m, per + side + j] = jnp.where(j == per * h + m, 0.0, big)
            if j < side - per:
                take[per + j, per + side + j] = 0.0

    @pl.when(h == half - 1)
    def _():
        place = jnp.int32(0)
        for i in range(side):
            inside = ((set_out >> i) & 1) == 1
            at = place

            @pl.when(inside)
            def _():
                send[at, i] = 0.0

            place = place + jnp.where(inside, 1, 0)
        for t in range(side):
            inside = (rows_out[t] & ~set_out) != 0
            at = place

            @pl.when(inside)
            def _():
                for i in range(side):
                    send[at, i] = edge(mode_of(~left, t), mode_of(left, i))

            place = place + jnp.where(inside, 1, 0)
        row_of = [per + t if t < side - per else t - (side - per) for t in range(side)]
        place = jnp.int32(0)
        for i in range(side):
            inside = ((set_in >> i) & 1) == 1
            at = place

            @pl.when(inside)
            def _():
                for t in range(side):
                    take[row_of[t], per + side + at] = edge(mode_of(left, t), mode_of(~left, i))

            place = place + jnp.where(inside, 1, 0)
        for t in range(side):
            inside = (rows_in[t] & ~set_in) != 0
            at = place

            @pl.when(inside)
            def _():
                take[row_of[t], per + side + at] = 0.0

            place = place + jnp.where(inside, 1, 0)


def weno_cells(u, count):
    d = [u[k + 1] - u[k] for k in range(count + 5)]
    e = [d[k + 1] - d[k] for k in range(count + 4)]
    e3 = [3.0 * e[k] for k in range(count + 4)]
    fs = [e[k + 1] - e[k] for k in range(count + 3)]
    g = [(13.0 / 3.0) * (f * f) + 4.0 * epsilon for f in fs]

    def squared(x, k):
        s = g[k] + x * x
        return s * s

    first = {k: squared(e[k] - e3[k + 1], k) for k in range(0, count + 1)}
    second = {k: squared(e[k] + e[k + 1], k) for k in range(1, count + 2)}
    third = {k: squared(e3[k] - e[k + 1], k) for k in range(2, count + 3)}

    def mix(a, b, c, x, y, w):
        wa = b * c
        wb = 6.0 * (a * c)
        wc = 3.0 * (a * b)
        return (wa * x + wb * y + wc * w) * pl.reciprocal(6.0 * (wa + wb + wc), approx=True)

    out = []
    for i in range(count):
        minus = d[i + 2] + mix(
            first[i],
            second[i + 1],
            third[i + 2],
            5.0 * e[i + 1] - 2.0 * e[i],
            e[i + 1] + 2.0 * e[i + 2],
            4.0 * e[i + 2] - e[i + 3],
        )
        plus = d[i + 3] - mix(
            third[i + 3],
            second[i + 2],
            first[i + 1],
            5.0 * e[i + 3] - 2.0 * e[i + 4],
            e[i + 3] + 2.0 * e[i + 2],
            4.0 * e[i + 2] - e[i + 1],
        )
        out.append((minus, plus))
    return out


def section_kernel(
    n, gx_count, gy_count, slots,
    coef, send_tab, take_tab, vals_hbm, out,
    vals, cells, fresh, outer_rx, inner_rx, in_slot, out_slot,
    load_sem, halo_send, halo_recv, in_send, in_recv, out_send, out_recv,
):
    per, rows, deep, lanes = vals.shape
    planes = cells.shape[0]
    chunks, _, _, width, _ = fresh.shape
    parts = chunks // rows
    cols = parts * width
    depth = deep // cols
    tiles = width // TILE
    half = n // 2
    side = per * half
    z, left, h = line_place(n)
    gx, gy = lax.axis_index("gx"), lax.axis_index("gy")
    inner_z = jnp.where(left, z + 1, z - 1)
    outer_z = jnp.where(left, z - 1, z + 1)

    groups = [(REACH, rows - 2 * REACH), (rows - REACH, REACH), (0, REACH)]

    def load(g):
        lo, size = groups[g]
        return pltpu.make_async_copy(
            vals_hbm.at[:, pl.ds(lo, size)], vals.at[:, pl.ds(lo, size)], load_sem.at[g]
        )

    for g in range(3):
        load(g).start()

    has = [gx > 0, gx < gx_count - 1, gy > 0, gy < gy_count - 1]
    barrier = pltpu.get_barrier_semaphore()
    peers = [
        (has[0], {"gx": gx - 1}),
        (has[1], {"gx": gx + 1}),
        (has[2], {"gy": gy - 1}),
        (has[3], {"gy": gy + 1}),
        (h > 0, {"mode": outer_z}),
        (h >= 0, {"mode": inner_z}),
    ]
    for there, who in peers:
        @pl.when(there)
        def _():
            pl.semaphore_signal(barrier, inc=1, device_id=who, device_id_type=MESH)

    for k, (there, lo) in enumerate([(has[0], 0), (has[1], REACH + rows)]):
        @pl.when(~there)
        def _():
            cells[:, :, lo : lo + REACH] = jnp.zeros(
                (planes, per, REACH) + cells.shape[3:], jnp.float32
            )
    for k, (there, lo) in enumerate([(has[2], 0), (has[3], PAD + cols)]):
        @pl.when(~there)
        def _():
            cells[:, :, REACH : REACH + rows, lo : lo + PAD] = jnp.zeros(
                (planes, per, rows, PAD, lanes), jnp.float32
            )

    def pack(i, carry):
        for m in range(per):
            for p in range(planes):
                cells[p, m, REACH + i, PAD : PAD + cols] = vals[
                    m, i, pl.ds(REACH + p, cols, stride=depth)
                ]
        return carry

    def pack_group(g):
        lo, size = groups[g]
        load(g).wait()
        lax.fori_loop(lo, lo + size, pack, 0)

    pack_group(0)
    met = sum(there.astype(jnp.int32) for there, _ in peers)
    pl.semaphore_wait(barrier, met)

    def cut(r, r_size, c, c_size):
        return cells.at[:, :, pl.ds(r, r_size), pl.ds(c, c_size)]

    def halo_copy(number, k, src, dst):
        return pltpu.make_async_remote_copy(
            src_ref=src,
            dst_ref=dst,
            send_sem=halo_send.at[number],
            recv_sem=halo_recv.at[number],
            device_id=peers[k][1],
            device_id_type=MESH,
        )

    def first_halo(k):
        src, dst = ((REACH, REACH + rows), (rows, 0))[k]
        return halo_copy(
            k, k, cut(src, REACH, PAD, cols), cut(dst, REACH, PAD, cols)
        )

    def second_halo(g, k):
        src, dst = ((PAD, PAD + cols), (cols, 0))[k - 2]
        lo, size = groups[g]
        return halo_copy(
            2 * g + k, k, cut(REACH + lo, size, src, PAD), cut(REACH + lo, size, dst, PAD)
        )

    def start_second(g):
        for k in (2, 3):
            @pl.when(has[k])
            def _():
                second_halo(g, k).start()

    def wait_second(g):
        for k in (2, 3):
            @pl.when(has[k])
            def _():
                second_halo(g, 5 - k).wait_recv()

    start_second(0)
    pack_group(1)
    pack_group(2)
    for k in (1, 0):
        @pl.when(has[k])
        def _():
            first_halo(k).start()
    start_second(1)
    start_second(2)
    wait_second(0)

    lane = lax.broadcasted_iota(jnp.int32, (TILE, lanes), 1).astype(jnp.float32)
    heading = 2.0 * jnp.pi * lane / lanes
    cosine, sine = jnp.cos(heading), jnp.sin(heading)
    top = 1.0 + 0.5 * (planes - 1)

    def chunk_at(s):
        return lax.rem(s // parts + REACH, rows) * parts + lax.rem(s, parts)

    def update_chunk(chunk):
        row = chunk // parts
        origin = lax.rem(chunk, parts) * width
        for m in range(per):
            shift, raw, accel = coef[m, 0], coef[m, 1], coef[m, 2]
            turn = 0.5 + jnp.abs(raw)
            side_one = 0.5 * (top + jnp.abs(shift))
            side_four = 0.5 * jnp.abs(accel)

            def tile(t, carry):
                base = pl.multiple_of(origin + t * TILE, TILE)
                here = pl.ds(pl.multiple_of(t * TILE, TILE), TILE)
                stack = [
                    vals[m, row, pl.ds(base * depth + j, TILE, stride=depth)]
                    for j in range(planes + 2 * REACH)
                ]
                four = weno_cells(stack, planes)
                for p in range(planes):
                    speed = 1.0 + 0.5 * p
                    centre = stack[REACH + p]
                    lane_shift = [
                        centre if k == REACH else pltpu.roll(centre, (REACH - k) % lanes, 1)
                        for k in range(2 * REACH + 1)
                    ]
                    one = weno_cells(
                        [
                            cells[p, m, row + k, pl.ds(base + PAD, TILE)]
                            for k in range(2 * REACH + 1)
                        ],
                        1,
                    )[0]
                    two = weno_cells(
                        [
                            cells[p, m, row + REACH, pl.ds(base + (PAD - REACH + k), TILE)]
                            for k in range(2 * REACH + 1)
                        ],
                        1,
                    )[0]
                    three = weno_cells(lane_shift, 1)[0]
                    total = (0.5 * (speed * cosine - shift)) * (one[0] + one[1])
                    total = total - side_one * (one[1] - one[0])
                    total = total + (0.5 * speed * sine) * (two[0] + two[1])
                    total = total - (0.5 * top) * (two[1] - two[0])
                    total = total + (0.5 * turn) * (
                        jnp.abs(three[0] + three[1]) - (three[1] - three[0])
                    )
                    total = total + (0.5 * accel) * (four[p][0] + four[p][1])
                    total = total - side_four * (four[p][1] - four[p][0])
                    fresh[chunk, m, p, here] = centre - time_step * total
                return carry

            lax.fori_loop(0, tiles, tile, 0)

    def inward_copies(hh, chunk):
        if hh == half - 1:
            return [
                pltpu.make_async_remote_copy(
                    src_ref=in_slot.at[chunk],
                    dst_ref=inner_rx.at[chunk, pl.ds(0, slots)],
                    send_sem=in_send.at[chunk, 0],
                    recv_sem=out_recv.at[chunk],
                    device_id={"mode": inner_z},
                    device_id_type=MESH,
                )
            ]
        copies = [
            pltpu.make_async_remote_copy(
                src_ref=fresh.at[chunk],
                dst_ref=outer_rx.at[chunk, pl.ds(per * hh, per)],
                send_sem=in_send.at[chunk, 0],
                recv_sem=in_recv.at[chunk, 0],
                device_id={"mode": inner_z},
                device_id_type=MESH,
            )
        ]
        if hh > 0:
            copies.append(
                pltpu.make_async_remote_copy(
                    src_ref=outer_rx.at[chunk, pl.ds(0, per * hh)],
                    dst_ref=outer_rx.at[chunk, pl.ds(0, per * hh)],
                    send_sem=in_send.at[chunk, 1],
                    recv_sem=in_recv.at[chunk, 1],
                    device_id={"mode": inner_z},
                    device_id_type=MESH,
                )
            )
        return copies

    def outward_copy(hh, chunk):
        return pltpu.make_async_remote_copy(
            src_ref=out_slot.at[chunk, pl.ds(0, per * hh)],
            dst_ref=inner_rx.at[chunk, pl.ds(0, per * hh)],
            send_sem=out_send.at[chunk],
            recv_sem=out_recv.at[chunk],
            device_id={"mode": outer_z},
            device_id_type=MESH,
        )

    def least(start, pairs):
        best = start
        for value, weight in pairs:
            best = value + weight if best is None else jnp.minimum(best, value + weight)
        return best

    def each_stage(body):
        for hh in range(half):
            @pl.when(h == hh)
            def _():
                body(hh)

    blocks = width // BLOCK

    def inward(hh, chunk):
        if hh > 0:
            for copy in inward_copies(hh - 1, chunk):
                copy.wait_recv()
        if hh == half - 1:
            def block(b, carry):
                span = pl.ds(pl.multiple_of(b * BLOCK, BLOCK), BLOCK)
                for p in range(planes):
                    given = [outer_rx[chunk, i, p, span] for i in range(per * hh)]
                    given += [fresh[chunk, m, p, span] for m in range(per)]
                    for j in range(slots):
                        in_slot[chunk, j, p, span] = least(
                            None, [(given[i], send_tab[j, i]) for i in range(side)]
                        )
                return carry

            lax.fori_loop(0, blocks, block, 0)
        for copy in inward_copies(hh, chunk):
            copy.start()

    def outward(hh, chunk):
        mid = hh == half - 1
        arrived = slots if mid else per * (hh + 1)
        if mid:
            inward_copies(hh, chunk)[0].wait_recv()
        else:
            outward_copy(hh + 1, chunk).wait_recv()

        def block(b, carry):
            start = pl.multiple_of(b * BLOCK, BLOCK)
            span = pl.ds(start, BLOCK)
            for p in range(planes):
                own = [fresh[chunk, m, p, span] for m in range(per)]
                outer = [outer_rx[chunk, i, p, span] for i in range(per * hh)]
                inner = [inner_rx[chunk, j, p, span] for j in range(arrived)]
                base = per + side
                for j in range(per * hh):
                    pairs = [(own[m], take_tab[per + j, m]) for m in range(per)]
                    if mid:
                        pairs += [
                            (inner[k], take_tab[per + j, base + k]) for k in range(arrived)
                        ]
                        out_slot[chunk, j, p, span] = least(None, pairs)
                    else:
                        out_slot[chunk, j, p, span] = least(inner[j], pairs)
                for m in range(per):
                    pairs = [(own[o], take_tab[m, o]) for o in range(per) if o != m]
                    pairs += [(outer[i], take_tab[m, per + i]) for i in range(per * hh)]
                    if mid:
                        pairs += [(inner[k], take_tab[m, base + k]) for k in range(arrived)]
                        best = least(own[m], pairs)
                    else:
                        best = least(jnp.minimum(own[m], inner[per * hh + m]), pairs)
                    at = (lax.rem(chunk, parts) * width + start) * planes + p
                    out[m, chunk // parts, pl.ds(at, BLOCK, stride=planes)] = best
            return carry

        lax.fori_loop(0, blocks, block, 0)
        if hh > 0:
            outward_copy(hh, chunk).start()

    in_lag = [IN_LAG * hh for hh in range(half)]
    out_lag = [
        chunks if hh == 0 and half > 1 else in_lag[hh] + OUT_LAG * (half - hh)
        for hh in range(half)
    ]

    def step(s, carry):
        for g, k, at in ((1, 0, rows - 2 * REACH), (2, 1, rows - REACH)):
            @pl.when(s == at * parts)
            def _():
                wait_second(g)

                @pl.when(has[1 - k])
                def _():
                    first_halo(k).wait_recv()

        @pl.when(s < chunks)
        def _():
            update_chunk(chunk_at(s))

        def stage(hh):
            @pl.when((s >= in_lag[hh]) & (s < chunks + in_lag[hh]))
            def _():
                inward(hh, chunk_at(s - in_lag[hh]))

            @pl.when((s >= out_lag[hh]) & (s < chunks + out_lag[hh]))
            def _():
                outward(hh, chunk_at(s - out_lag[hh]))

        each_stage(stage)
        return carry

    lax.fori_loop(0, chunks + max(in_lag + out_lag), step, 0)

    for k in range(4):
        @pl.when(has[k])
        def _():
            if k < 2:
                first_halo(k).wait_send()
            else:
                for g in range(3):
                    second_halo(g, k).wait_send()

    def finish(chunk, carry):
        def stage(hh):
            for copy in inward_copies(hh, chunk):
                copy.wait_send()
            if hh > 0:
                outward_copy(hh, chunk).wait_send()

        each_stage(stage)
        return carry

    lax.fori_loop(0, chunks, finish, 0)


def smem():
    return pl.BlockSpec(memory_space=pltpu.SMEM)


def shards(n, gx_count, gy_count, values, coef_table, mode_coef, switch_mask, switch_cost):
    per, rows, cols, depth, lanes = values.shape
    planes = depth - 2 * REACH
    side = per * (n // 2)
    f32 = jnp.float32
    coef, send_tab, take_tab, rank = pl.pallas_call(
        functools.partial(plan_kernel, n, per),
        out_shape=(
            jax.ShapeDtypeStruct((per, 3), f32),
            jax.ShapeDtypeStruct((side, side), f32),
            jax.ShapeDtypeStruct((per + side, per + 2 * side), f32),
            jax.ShapeDtypeStruct((1,), jnp.int32),
        ),
        in_specs=[smem()] * 4,
        out_specs=(smem(),) * 4,
        name="plan",
    )(switch_mask, switch_cost, coef_table, mode_coef)
    parts = 2 if cols % (2 * TILE) == 0 else 1
    chunks = rows * parts
    piece = (planes, cols // parts, lanes)
    dma = pltpu.SemaphoreType.DMA
    def section_with(slots, number):
        return pl.pallas_call(
            functools.partial(section_kernel, n, gx_count, gy_count, slots),
            out_shape=jax.ShapeDtypeStruct((per, rows, cols * planes, lanes), f32),
            in_specs=[smem()] * 3 + [pl.BlockSpec(memory_space=pl.ANY)],
            out_specs=pl.BlockSpec(memory_space=pltpu.VMEM),
            scratch_shapes=[
                pltpu.VMEM((per, rows, cols * depth, lanes), f32),
                pltpu.VMEM((planes, per, rows + 2 * REACH, cols + 2 * PAD, lanes), f32),
                pltpu.VMEM((chunks, per) + piece, f32),
                pltpu.VMEM((chunks, max(side - per, 1)) + piece, f32),
                pltpu.VMEM((chunks, side) + piece, f32),
                pltpu.VMEM((chunks, slots) + piece, f32),
                pltpu.VMEM((chunks, max(side - per, 1)) + piece, f32),
                dma((3,)),
                dma((8,)),
                dma((8,)),
                dma((chunks, 2)),
                dma((chunks, 2)),
                dma((chunks,)),
                dma((chunks,)),
            ],
            compiler_params=pltpu.CompilerParams(
                collective_id=number, has_side_effects=True, vmem_limit_bytes=58 * 1024 * 1024
            ),
            name="section",
        )

    sizes = sorted({max(side // 2, 1), max(3 * side // 4, 1), side})
    pick = sum((rank[0] > size).astype(jnp.int32) for size in sizes[:-1])
    out = lax.switch(
        pick,
        [section_with(size, number) for number, size in enumerate(sizes)],
        coef,
        send_tab,
        take_tab,
        values.reshape(per, rows, cols * depth, lanes),
    )
    return out.reshape(per, rows, cols, planes, lanes)


def solution(mesh):
    in_specs = (P("mode", "gx", "gy", None, None), P(), P("mode"), P(), P())
    out_specs = P("mode", "gx", "gy", None, None)
    body = functools.partial(shards, mesh.shape["mode"], mesh.shape["gx"], mesh.shape["gy"])
    return jax.shard_map(body, mesh=mesh, in_specs=in_specs, out_specs=out_specs, check_vma=False)
```

```python
import functools

import jax
import jax.numpy as jnp
from jax import lax
from jax.experimental import pallas as pl
from jax.experimental.pallas import tpu as pltpu
from jax.sharding import PartitionSpec as P

epsilon = 1e-06
time_step = 0.1
MESH = pl.DeviceIdType.MESH
REACH = 3
PAD = 8
TILE = 8
BLOCK = 8
IN_LAG = 2
OUT_LAG_FEW, OUT_LAG_MANY = 4, 6


def line_place(n):
    z = lax.axis_index("mode")
    half = n // 2
    left = z < half
    h = jnp.where(left, z, n - 1 - z)
    return z, left, h


def plan_kernel(n, per, mask, cost, table, kinds, coef, send, take, rank):
    z, left, h = line_place(n)
    half = n // 2
    side = per * half
    big = jnp.float32(jnp.inf)

    def mode_of(on_left, i):
        dev = i // per
        return per * jnp.where(on_left, dev, n - 1 - dev) + i % per

    def edge(target, source):
        ok = (mask[target, source] == 1) & (target != source)
        return jnp.where(ok, cost[target, source], big)

    for m in range(per):
        kind = kinds[m]
        for j in range(3):
            coef[m, j] = table[j, kind]

    def cover(from_left):
        rows = []
        for t in range(side):
            bits = jnp.int32(0)
            for i in range(side):
                hit = mask[mode_of(~from_left, t), mode_of(from_left, i)] == 1
                bits = bits + jnp.where(hit, jnp.int32(1 << i), jnp.int32(0))
            rows.append(bits)

        def size_of(chosen):
            total = jnp.int32(0)
            for i in range(side):
                total = total + ((chosen >> i) & 1)
            for t in range(side):
                total = total + jnp.where((rows[t] & ~chosen) != 0, 1, 0)
            return total

        everything = jnp.int32((1 << side) - 1)

        def better(s, best):
            size = size_of(s)
            win = size < best[1]
            return jnp.where(win, s, best[0]), jnp.where(win, size, best[1])

        chosen, size = lax.fori_loop(
            0, (1 << side) - 1, better, (everything, jnp.int32(side))
        )
        return rows, chosen, size

    for j in range(side):
        for i in range(side):
            send[j, i] = big
    for row in range(per + side):
        for col in range(per + 2 * side):
            take[row, col] = big

    own = [mode_of(left, per * h + m) for m in range(per)]
    for m in range(per):
        for o in range(per):
            take[m, o] = edge(own[m], own[o])
        for i in range(side - per):
            take[m, per + i] = edge(own[m], mode_of(left, i))
    for j in range(side - per):
        for o in range(per):
            take[per + j, o] = edge(mode_of(left, j), own[o])

    rows_out, set_out, size_out = cover(left)
    rows_in, set_in, size_in = cover(~left)
    rank[0] = jnp.maximum(size_out, size_in)

    @pl.when(h < half - 1)
    def _():
        for j in range(side):
            for m in range(per):
                take[m, per + side + j] = jnp.where(j == per * h + m, 0.0, big)
            if j < side - per:
                take[per + j, per + side + j] = 0.0

    @pl.when(h == half - 1)
    def _():
        place = jnp.int32(0)
        for i in range(side):
            inside = ((set_out >> i) & 1) == 1
            at = place

            @pl.when(inside)
            def _():
                send[at, i] = 0.0

            place = place + jnp.where(inside, 1, 0)
        for t in range(side):
            inside = (rows_out[t] & ~set_out) != 0
            at = place

            @pl.when(inside)
            def _():
                for i in range(side):
                    send[at, i] = edge(mode_of(~left, t), mode_of(left, i))

            place = place + jnp.where(inside, 1, 0)
        row_of = [per + t if t < side - per else t - (side - per) for t in range(side)]
        place = jnp.int32(0)
        for i in range(side):
            inside = ((set_in >> i) & 1) == 1
            at = place

            @pl.when(inside)
            def _():
                for t in range(side):
                    take[row_of[t], per + side + at] = edge(mode_of(left, t), mode_of(~left, i))

            place = place + jnp.where(inside, 1, 0)
        for t in range(side):
            inside = (rows_in[t] & ~set_in) != 0
            at = place

            @pl.when(inside)
            def _():
                take[row_of[t], per + side + at] = 0.0

            place = place + jnp.where(inside, 1, 0)


def weno_cells(u, count):
    d = [u[k + 1] - u[k] for k in range(count + 5)]
    e = [d[k + 1] - d[k] for k in range(count + 4)]
    e3 = [3.0 * e[k] for k in range(count + 4)]
    fs = [e[k + 1] - e[k] for k in range(count + 3)]
    g = [(13.0 / 3.0) * (f * f) + 4.0 * epsilon for f in fs]

    def squared(x, k):
        s = g[k] + x * x
        return s * s

    first = {k: squared(e[k] - e3[k + 1], k) for k in range(0, count + 1)}
    second = {k: squared(e[k] + e[k + 1], k) for k in range(1, count + 2)}
    third = {k: squared(e3[k] - e[k + 1], k) for k in range(2, count + 3)}

    def mix(a, b, c, x, y, w):
        wa = b * c
        wb = 6.0 * (a * c)
        wc = 3.0 * (a * b)
        return (wa * x + wb * y + wc * w) * pl.reciprocal(6.0 * (wa + wb + wc), approx=True)

    out = []
    for i in range(count):
        minus = d[i + 2] + mix(
            first[i],
            second[i + 1],
            third[i + 2],
            5.0 * e[i + 1] - 2.0 * e[i],
            e[i + 1] + 2.0 * e[i + 2],
            4.0 * e[i + 2] - e[i + 3],
        )
        plus = d[i + 3] - mix(
            third[i + 3],
            second[i + 2],
            first[i + 1],
            5.0 * e[i + 3] - 2.0 * e[i + 4],
            e[i + 3] + 2.0 * e[i + 2],
            4.0 * e[i + 2] - e[i + 1],
        )
        out.append((minus, plus))
    return out


def section_kernel(
    n, gx_count, gy_count, slots,
    coef, send_tab, take_tab, vals_hbm, out,
    vals, cells, fresh, outer_rx, inner_rx, in_slot, out_slot,
    load_sem, halo_send, halo_recv, in_send, in_recv, out_send, out_recv,
):
    per, rows, deep, lanes = vals.shape
    planes = cells.shape[0]
    chunks, _, _, width, _ = fresh.shape
    parts = chunks // rows
    cols = parts * width
    depth = deep // cols
    tiles = width // TILE
    half = n // 2
    side = per * half
    z, left, h = line_place(n)
    gx, gy = lax.axis_index("gx"), lax.axis_index("gy")
    inner_z = jnp.where(left, z + 1, z - 1)
    outer_z = jnp.where(left, z - 1, z + 1)

    groups = [(REACH, rows - 2 * REACH), (rows - REACH, REACH), (0, REACH)]

    def load(g):
        lo, size = groups[g]
        return pltpu.make_async_copy(
            vals_hbm.at[:, pl.ds(lo, size)], vals.at[:, pl.ds(lo, size)], load_sem.at[g]
        )

    for g in range(3):
        load(g).start()

    has = [gx > 0, gx < gx_count - 1, gy > 0, gy < gy_count - 1]
    barrier = pltpu.get_barrier_semaphore()
    peers = [
        (has[0], {"gx": gx - 1}),
        (has[1], {"gx": gx + 1}),
        (has[2], {"gy": gy - 1}),
        (has[3], {"gy": gy + 1}),
        (h > 0, {"mode": outer_z}),
        (h >= 0, {"mode": inner_z}),
    ]
    for there, who in peers:
        @pl.when(there)
        def _():
            pl.semaphore_signal(barrier, inc=1, device_id=who, device_id_type=MESH)

    for k, (there, lo) in enumerate([(has[0], 0), (has[1], REACH + rows)]):
        @pl.when(~there)
        def _():
            cells[:, :, lo : lo + REACH] = jnp.zeros(
                (planes, per, REACH) + cells.shape[3:], jnp.float32
            )
    for k, (there, lo) in enumerate([(has[2], 0), (has[3], PAD + cols)]):
        @pl.when(~there)
        def _():
            cells[:, :, REACH : REACH + rows, lo : lo + PAD] = jnp.zeros(
                (planes, per, rows, PAD, lanes), jnp.float32
            )

    def pack(i, carry):
        for m in range(per):
            for p in range(planes):
                cells[p, m, REACH + i, PAD : PAD + cols] = vals[
                    m, i, pl.ds(REACH + p, cols, stride=depth)
                ]
        return carry

    def pack_group(g):
        lo, size = groups[g]
        load(g).wait()
        lax.fori_loop(lo, lo + size, pack, 0)

    pack_group(0)
    met = sum(there.astype(jnp.int32) for there, _ in peers)
    pl.semaphore_wait(barrier, met)

    def cut(r, r_size, c, c_size):
        return cells.at[:, :, pl.ds(r, r_size), pl.ds(c, c_size)]

    def halo_copy(number, k, src, dst):
        return pltpu.make_async_remote_copy(
            src_ref=src,
            dst_ref=dst,
            send_sem=halo_send.at[number],
            recv_sem=halo_recv.at[number],
            device_id=peers[k][1],
            device_id_type=MESH,
        )

    def first_halo(k):
        src, dst = ((REACH, REACH + rows), (rows, 0))[k]
        return halo_copy(
            k, k, cut(src, REACH, PAD, cols), cut(dst, REACH, PAD, cols)
        )

    def second_halo(g, k):
        src, dst = ((PAD, PAD + cols), (cols, 0))[k - 2]
        lo, size = groups[g]
        return halo_copy(
            2 * g + k, k, cut(REACH + lo, size, src, PAD), cut(REACH + lo, size, dst, PAD)
        )

    def start_second(g):
        for k in (2, 3):
            @pl.when(has[k])
            def _():
                second_halo(g, k).start()

    def wait_second(g):
        for k in (2, 3):
            @pl.when(has[k])
            def _():
                second_halo(g, 5 - k).wait_recv()

    start_second(0)
    pack_group(1)
    pack_group(2)
    for k in (1, 0):
        @pl.when(has[k])
        def _():
            first_halo(k).start()
    start_second(1)
    start_second(2)
    wait_second(0)

    lane = lax.broadcasted_iota(jnp.int32, (TILE, lanes), 1).astype(jnp.float32)
    heading = 2.0 * jnp.pi * lane / lanes
    cosine, sine = jnp.cos(heading), jnp.sin(heading)
    top = 1.0 + 0.5 * (planes - 1)

    def chunk_at(s):
        return lax.rem(s // parts + REACH, rows) * parts + lax.rem(s, parts)

    def update_chunk(chunk):
        row = chunk // parts
        origin = lax.rem(chunk, parts) * width
        for m in range(per):
            shift, raw, accel = coef[m, 0], coef[m, 1], coef[m, 2]
            turn = 0.5 + jnp.abs(raw)
            side_one = 0.5 * (top + jnp.abs(shift))
            side_four = 0.5 * jnp.abs(accel)

            def tile(t, carry):
                base = pl.multiple_of(origin + t * TILE, TILE)
                here = pl.ds(pl.multiple_of(t * TILE, TILE), TILE)
                stack = [
                    vals[m, row, pl.ds(base * depth + j, TILE, stride=depth)]
                    for j in range(planes + 2 * REACH)
                ]
                four = weno_cells(stack, planes)
                for p in range(planes):
                    speed = 1.0 + 0.5 * p
                    centre = stack[REACH + p]
                    lane_shift = [
                        centre if k == REACH else pltpu.roll(centre, (REACH - k) % lanes, 1)
                        for k in range(2 * REACH + 1)
                    ]
                    one = weno_cells(
                        [
                            cells[p, m, row + k, pl.ds(base + PAD, TILE)]
                            for k in range(2 * REACH + 1)
                        ],
                        1,
                    )[0]
                    two = weno_cells(
                        [
                            cells[p, m, row + REACH, pl.ds(base + (PAD - REACH + k), TILE)]
                            for k in range(2 * REACH + 1)
                        ],
                        1,
                    )[0]
                    three = weno_cells(lane_shift, 1)[0]
                    total = (0.5 * (speed * cosine - shift)) * (one[0] + one[1])
                    total = total - side_one * (one[1] - one[0])
                    total = total + (0.5 * speed * sine) * (two[0] + two[1])
                    total = total - (0.5 * top) * (two[1] - two[0])
                    total = total + (0.5 * turn) * (
                        jnp.abs(three[0] + three[1]) - (three[1] - three[0])
                    )
                    total = total + (0.5 * accel) * (four[p][0] + four[p][1])
                    total = total - side_four * (four[p][1] - four[p][0])
                    fresh[chunk, m, p, here] = centre - time_step * total
                return carry

            lax.fori_loop(0, tiles, tile, 0)

    def inward_copies(hh, chunk):
        if hh == half - 1:
            return [
                pltpu.make_async_remote_copy(
                    src_ref=in_slot.at[chunk],
                    dst_ref=inner_rx.at[chunk, pl.ds(0, slots)],
                    send_sem=in_send.at[chunk, 0],
                    recv_sem=out_recv.at[chunk],
                    device_id={"mode": inner_z},
                    device_id_type=MESH,
                )
            ]
        copies = [
            pltpu.make_async_remote_copy(
                src_ref=fresh.at[chunk],
                dst_ref=outer_rx.at[chunk, pl.ds(per * hh, per)],
                send_sem=in_send.at[chunk, 0],
                recv_sem=in_recv.at[chunk, 0],
                device_id={"mode": inner_z},
                device_id_type=MESH,
            )
        ]
        if hh > 0:
            copies.append(
                pltpu.make_async_remote_copy(
                    src_ref=outer_rx.at[chunk, pl.ds(0, per * hh)],
                    dst_ref=outer_rx.at[chunk, pl.ds(0, per * hh)],
                    send_sem=in_send.at[chunk, 1],
                    recv_sem=in_recv.at[chunk, 1],
                    device_id={"mode": inner_z},
                    device_id_type=MESH,
                )
            )
        return copies

    def outward_copy(hh, chunk):
        return pltpu.make_async_remote_copy(
            src_ref=out_slot.at[chunk, pl.ds(0, per * hh)],
            dst_ref=inner_rx.at[chunk, pl.ds(0, per * hh)],
            send_sem=out_send.at[chunk],
            recv_sem=out_recv.at[chunk],
            device_id={"mode": outer_z},
            device_id_type=MESH,
        )

    def least(start, pairs):
        best = start
        for value, weight in pairs:
            best = value + weight if best is None else jnp.minimum(best, value + weight)
        return best

    def each_stage(body):
        for hh in range(half):
            @pl.when(h == hh)
            def _():
                body(hh)

    blocks = width // BLOCK

    def inward(hh, chunk):
        if hh > 0:
            for copy in inward_copies(hh - 1, chunk):
                copy.wait_recv()
        if hh == half - 1:
            def block(b, carry):
                span = pl.ds(pl.multiple_of(b * BLOCK, BLOCK), BLOCK)
                for p in range(planes):
                    given = [outer_rx[chunk, i, p, span] for i in range(per * hh)]
                    given += [fresh[chunk, m, p, span] for m in range(per)]
                    for j in range(slots):
                        in_slot[chunk, j, p, span] = least(
                            None, [(given[i], send_tab[j, i]) for i in range(side)]
                        )
                return carry

            lax.fori_loop(0, blocks, block, 0)
        for copy in inward_copies(hh, chunk):
            copy.start()

    def outward(hh, chunk):
        mid = hh == half - 1
        arrived = slots if mid else per * (hh + 1)
        if mid:
            inward_copies(hh, chunk)[0].wait_recv()
        else:
            outward_copy(hh + 1, chunk).wait_recv()

        def block(b, carry):
            start = pl.multiple_of(b * BLOCK, BLOCK)
            span = pl.ds(start, BLOCK)
            for p in range(planes):
                own = [fresh[chunk, m, p, span] for m in range(per)]
                outer = [outer_rx[chunk, i, p, span] for i in range(per * hh)]
                inner = [inner_rx[chunk, j, p, span] for j in range(arrived)]
                base = per + side
                for j in range(per * hh):
                    pairs = [(own[m], take_tab[per + j, m]) for m in range(per)]
                    if mid:
                        pairs += [
                            (inner[k], take_tab[per + j, base + k]) for k in range(arrived)
                        ]
                        out_slot[chunk, j, p, span] = least(None, pairs)
                    else:
                        out_slot[chunk, j, p, span] = least(inner[j], pairs)
                for m in range(per):
                    pairs = [(own[o], take_tab[m, o]) for o in range(per) if o != m]
                    pairs += [(outer[i], take_tab[m, per + i]) for i in range(per * hh)]
                    if mid:
                        pairs += [(inner[k], take_tab[m, base + k]) for k in range(arrived)]
                        best = least(own[m], pairs)
                    else:
                        best = least(jnp.minimum(own[m], inner[per * hh + m]), pairs)
                    at = (lax.rem(chunk, parts) * width + start) * planes + p
                    out[m, chunk // parts, pl.ds(at, BLOCK, stride=planes)] = best
            return carry

        lax.fori_loop(0, blocks, block, 0)
        if hh > 0:
            outward_copy(hh, chunk).start()

    in_lag = [IN_LAG * hh for hh in range(half)]
    out_wait = OUT_LAG_FEW if slots <= side // 2 else OUT_LAG_MANY
    out_lag = [
        chunks if hh == 0 and half > 1 else in_lag[hh] + out_wait * (half - hh)
        for hh in range(half)
    ]

    def step(s, carry):
        for g, k, at in ((1, 0, rows - 2 * REACH), (2, 1, rows - REACH)):
            @pl.when(s == at * parts)
            def _():
                wait_second(g)

                @pl.when(has[1 - k])
                def _():
                    first_halo(k).wait_recv()

        @pl.when(s < chunks)
        def _():
            update_chunk(chunk_at(s))

        def stage(hh):
            @pl.when((s >= in_lag[hh]) & (s < chunks + in_lag[hh]))
            def _():
                inward(hh, chunk_at(s - in_lag[hh]))

            @pl.when((s >= out_lag[hh]) & (s < chunks + out_lag[hh]))
            def _():
                outward(hh, chunk_at(s - out_lag[hh]))

        each_stage(stage)
        return carry

    lax.fori_loop(0, chunks + max(in_lag + out_lag), step, 0)

    for k in range(4):
        @pl.when(has[k])
        def _():
            if k < 2:
                first_halo(k).wait_send()
            else:
                for g in range(3):
                    second_halo(g, k).wait_send()

    def finish(chunk, carry):
        def stage(hh):
            for copy in inward_copies(hh, chunk):
                copy.wait_send()
            if hh > 0:
                outward_copy(hh, chunk).wait_send()

        each_stage(stage)
        return carry

    lax.fori_loop(0, chunks, finish, 0)


def smem():
    return pl.BlockSpec(memory_space=pltpu.SMEM)


def shards(n, gx_count, gy_count, values, coef_table, mode_coef, switch_mask, switch_cost):
    per, rows, cols, depth, lanes = values.shape
    planes = depth - 2 * REACH
    side = per * (n // 2)
    f32 = jnp.float32
    coef, send_tab, take_tab, rank = pl.pallas_call(
        functools.partial(plan_kernel, n, per),
        out_shape=(
            jax.ShapeDtypeStruct((per, 3), f32),
            jax.ShapeDtypeStruct((side, side), f32),
            jax.ShapeDtypeStruct((per + side, per + 2 * side), f32),
            jax.ShapeDtypeStruct((1,), jnp.int32),
        ),
        in_specs=[smem()] * 4,
        out_specs=(smem(),) * 4,
        name="plan",
    )(switch_mask, switch_cost, coef_table, mode_coef)
    parts = 2 if cols % (2 * TILE) == 0 else 1
    chunks = rows * parts
    piece = (planes, cols // parts, lanes)
    dma = pltpu.SemaphoreType.DMA
    def section_with(slots, number):
        return pl.pallas_call(
            functools.partial(section_kernel, n, gx_count, gy_count, slots),
            out_shape=jax.ShapeDtypeStruct((per, rows, cols * planes, lanes), f32),
            in_specs=[smem()] * 3 + [pl.BlockSpec(memory_space=pl.ANY)],
            out_specs=pl.BlockSpec(memory_space=pltpu.VMEM),
            scratch_shapes=[
                pltpu.VMEM((per, rows, cols * depth, lanes), f32),
                pltpu.VMEM((planes, per, rows + 2 * REACH, cols + 2 * PAD, lanes), f32),
                pltpu.VMEM((chunks, per) + piece, f32),
                pltpu.VMEM((chunks, max(side - per, 1)) + piece, f32),
                pltpu.VMEM((chunks, side) + piece, f32),
                pltpu.VMEM((chunks, slots) + piece, f32),
                pltpu.VMEM((chunks, max(side - per, 1)) + piece, f32),
                dma((3,)),
                dma((8,)),
                dma((8,)),
                dma((chunks, 2)),
                dma((chunks, 2)),
                dma((chunks,)),
                dma((chunks,)),
            ],
            compiler_params=pltpu.CompilerParams(
                collective_id=number, has_side_effects=True, vmem_limit_bytes=58 * 1024 * 1024
            ),
            name="section",
        )

    sizes = sorted({max(side // 2, 1), max(3 * side // 4, 1), side})
    pick = sum((rank[0] > size).astype(jnp.int32) for size in sizes[:-1])
    out = lax.switch(
        pick,
        [section_with(size, number) for number, size in enumerate(sizes)],
        coef,
        send_tab,
        take_tab,
        values.reshape(per, rows, cols * depth, lanes),
    )
    return out.reshape(per, rows, cols, planes, lanes)


def solution(mesh):
    in_specs = (P("mode", "gx", "gy", None, None), P(), P("mode"), P(), P())
    out_specs = P("mode", "gx", "gy", None, None)
    body = functools.partial(shards, mesh.shape["mode"], mesh.shape["gx"], mesh.shape["gy"])
    return jax.shard_map(body, mesh=mesh, in_specs=in_specs, out_specs=out_specs, check_vma=False)
```
